32 devices in a mesh: groups: 2 (over y), row: 2 (over x), col: 4 (over z), depth: 2 (over core).
Axes of the slice: x: 2, y: 2, z: 4, core: 2. Of those that a mesh axis runs over, the one named last changes fastest.
Arguments:
- inputs: bfloat16 [2048, 2304], P(('groups', 'row'), ('col', 'depth')), parts along dimension 0, may hold values from -6 to 6
- probe: bfloat16 [2048, 2304], P(('groups', 'row'), ('col', 'depth')), parts along dimension 0, may hold values from -6 to 6
- cotangent: bfloat16 [2048, 2304], P(('groups', 'row'), ('col', 'depth')), parts along dimension 0, may hold values from -6 to 6
- gate_weight: bfloat16 [2304, 9216], P('row', ('col', 'depth')), may hold values from -0.1875 to 0.1875
- up_weight: bfloat16 [2304, 9216], P('row', ('col', 'depth')), may hold values from -0.125 to 0.125
- down_weight: bfloat16 [9216, 2304], P(('col', 'depth'), 'row'), may hold values from -0.0625 to 0.0625
Outputs:
- hvp: bfloat16 [2048, 2304], P(('groups', 'row'), ('col', 'depth')), parts along dimension 0
The draws below stay inside these ranges and needn't reach their ends.
There are 2 independent parts, one for each index of `groups`. The reference program is written for one: setup_inputs(seed, part) draws one part's arguments, and reference() takes and returns one part's arrays. A program takes and returns all parts, laid end to end along the dimension named above; an argument that names none is the same for every part. Nothing has to cross between parts.
All inputs are finite; a program needn't handle non-finite values.
Results may differ from the reference program's by a relative error of at most 0.014.
Values may be sent and summed in bfloat16 or wider, within the bound.
A program may use at most 128 MiB of HBM per device.

```python
import jax
import jax.numpy as jnp
from jax import lax

D = 2304
FF = 9216
TOKENS = 1024
N_COL = 4
N_DEPTH = 2


def strengthened(entries, stream_key, source, target, blocks, factor):
    def block_of(position):
        return (jnp.arange(entries.shape[position]) // (entries.shape[position] // blocks)).reshape((-1,) + (1,) * (entries.ndim - 1 - position))

    first = jax.random.permutation(stream_key, blocks)[block_of(target)]
    other_side = (block_of(target) + blocks // 2) % blocks
    return jnp.where((block_of(source) == first) | (block_of(source) == other_side), factor * entries, entries)


def levels(rng, shape, split, smallest, largest):
    gain, own = 1.0, jax.random.fold_in(rng, 6)
    for axis_at, shards_of in split:
        steps = jnp.exp(jax.random.uniform(jax.random.fold_in(own, axis_at), (shards_of,), jnp.float32, smallest / len(split), largest / len(split)))
        gain = gain * jnp.repeat(steps, shape[axis_at] // shards_of).reshape([-1 if axis == axis_at else 1 for axis in range(len(shape))])
    return gain


def scatter_about(stream_key, extent, scale, reach, pieces=(), dtype=jnp.bfloat16):
    entries = jax.random.normal(stream_key, extent, jnp.float32) * scale
    if len(pieces) > 0:
        entries = levels(stream_key, extent, pieces, -0.22, 0.18) * entries
    return jnp.clip(entries, min=-reach, max=reach).astype(dtype)


def bell_draw_with(stream_key, shape, scale, reach, cuts, heavy, dtype=jnp.bfloat16):
    result = scale * jax.random.normal(stream_key, shape, jnp.float32)
    if cuts:
        result = result * levels(stream_key, shape, cuts, -0.22, 0.18)
    return jnp.clip(strengthened(result, jax.random.fold_in(stream_key, 3), *heavy), -reach, reach).astype(dtype)


def setup_inputs(seed: int = 0, part: int = 0) -> dict:
    streams_of = jax.random.split(jax.random.key(seed), 7)
    part_keys = jax.random.split(jax.random.fold_in(streams_of[6], part), 7)
    return {
        "inputs": scatter_about(part_keys[0], (TOKENS, D), 1.0, 6.0, ((0, 2), (1, 8))),
        "probe": scatter_about(part_keys[1], (TOKENS, D), 1.0, 6.0, ((0, 2), (1, 8))),
        "cotangent": scatter_about(part_keys[2], (TOKENS, D), 1.0, 6.0, ((0, 2), (1, 8))),
        "gate_weight": bell_draw_with(streams_of[3], (D, FF), D ** -0.5, 0.1875, ((0, 2), (1, 8)), (1, 0, 8, 2.0)),
        "up_weight": scatter_about(streams_of[4], (D, FF), D ** -0.5, 0.125, ((0, 2), (1, 8))),
        "down_weight": scatter_about(streams_of[5], (FF, D), FF ** -0.5, 0.0625, ((0, 8), (1, 2))),
    }


def gelu_tanh(value):
    return 0.5 * value * (1.0 + jnp.tanh(0.7978845608 * (value + 0.044715 * value * value * value)))


def gelu_slope(value):
    return jax.jvp(gelu_tanh, (value,), (jnp.ones_like(value),))[1]


def gelu_bend(value):
    return jax.jvp(gelu_slope, (value,), (jnp.ones_like(value),))[1]


def reference(inputs, probe, cotangent, gate_weight, up_weight, down_weight):
    pre_gate = jnp.dot(inputs, gate_weight, preferred_element_type=jnp.float32)
    pre_up = jnp.dot(inputs, up_weight, preferred_element_type=jnp.float32)
    tan_gate = jnp.dot(probe, gate_weight, preferred_element_type=jnp.float32)
    tan_up = jnp.dot(probe, up_weight, preferred_element_type=jnp.float32)
    back = lax.dot_general(cotangent, down_weight, (((1,), (1,)), ((), ())), preferred_element_type=jnp.float32)
    slope = gelu_slope(pre_gate)
    gate_part = (back * (tan_up * slope + pre_up * gelu_bend(pre_gate) * tan_gate)).astype(jnp.bfloat16)
    up_part = (back * slope * tan_gate).astype(jnp.bfloat16)
    blocks = N_COL * N_DEPTH
    width = FF // blocks

    def add_block(index, total):
        begin = index * width
        gate_block = lax.dynamic_slice_in_dim(gate_part, begin, width, 1)
        up_block = lax.dynamic_slice_in_dim(up_part, begin, width, 1)
        gate_cols = lax.dynamic_slice_in_dim(gate_weight, begin, width, 1)
        up_cols = lax.dynamic_slice_in_dim(up_weight, begin, width, 1)
        term = lax.dot_general(gate_block, gate_cols, (((1,), (1,)), ((), ())), preferred_element_type=jnp.float32)
        term = term + lax.dot_general(up_block, up_cols, (((1,), (1,)), ((), ())), preferred_element_type=jnp.float32)
        rounded = lax.optimization_barrier(term.astype(jnp.bfloat16))
        return total + rounded.astype(jnp.float32)

    total = lax.fori_loop(0, blocks, add_block, jnp.zeros((TOKENS, D), jnp.float32))
    return total.astype(jnp.bfloat16)
```

```python
import functools

import jax
import jax.numpy as jnp
from jax import lax
from jax.experimental import pallas as pl
from jax.experimental.pallas import tpu as pltpu
from jax.sharding import PartitionSpec as P

MESH = pl.DeviceIdType.MESH
F32, BF16 = jnp.float32, jnp.bfloat16
K0, K1 = 0.7978845608, 0.044715
PIECE = 128
WIDE = 256


def gelu_tanh(value):
    return 0.5 * value * (1.0 + jnp.tanh(K0 * (value + K1 * value * value * value)))


def gelu_slope(value):
    return jax.jvp(gelu_tanh, (value,), (jnp.ones_like(value),))[1]


def gelu_bend(value):
    return jax.jvp(gelu_slope, (value,), (jnp.ones_like(value),))[1]


def slope_and_bend(s):
    sq = s * s
    t = jnp.tanh(K0 * s * (1.0 + K1 * sq))
    du = K0 + (3.0 * K0 * K1) * sq
    e = 1.0 - t * t
    slope = 0.5 * (1.0 + t) + 0.5 * s * e * du
    bend = e * (K0 + (6.0 * K0 * K1) * sq - s * t * du * du)
    return slope, bend


def nt(a, b):
    return lax.dot_general(a, b, (((1,), (1,)), ((), ())), preferred_element_type=F32)


def nn(a, b):
    return jnp.dot(a, b, preferred_element_type=F32)


def kernel(
    n, acts_ref, gw_ref, uw_ref, dw_ref, out_ref,
    xt, xs, cot, own_g, own_u, own_d, far_g, far_u, far_d, acc,
    sib_out, sib_in, z_out, z_in,
    own_sem, xsend, xrecv, ysend, yrecv, rsend, rrecv, lsend, lrecv, ssend, srecv,
    qsend, qrecv, zsend, zrecv,
):
    g, r = lax.axis_index("groups"), lax.axis_index("row")
    c, d = lax.axis_index("col"), lax.axis_index("depth")
    half, hidden = gw_ref.shape
    part, tokens = acts_ref.shape[1:]
    pieces = hidden // PIECE
    hd = half // 2

    def at(gg=g, rr=r, cc=c, dd=d):
        return (gg, rr, cc, dd)

    x_dev, y_dev, sib = at(rr=1 - r), at(gg=1 - g), at(dd=1 - d)

    def rows_of(cc, dd):
        return pl.ds(pl.multiple_of((cc * 2 + dd) * part, 32), part)

    own_copies = [
        pltpu.make_async_copy(acts_ref, xt.at[:, rows_of(c, d), :], own_sem.at[0]),
        pltpu.make_async_copy(gw_ref, own_g, own_sem.at[1]),
        pltpu.make_async_copy(uw_ref, own_u, own_sem.at[2]),
        pltpu.make_async_copy(dw_ref, own_d, own_sem.at[3]),
    ]
    for cp in own_copies:
        cp.start()

    barrier = pltpu.get_barrier_semaphore()
    for dev in (x_dev, y_dev, sib):
        pl.semaphore_signal(barrier, inc=1, device_id=dev, device_id_type=MESH)
    for k in range(1, n):
        pl.semaphore_signal(
            barrier, inc=1, device_id=at(cc=lax.rem(c + k, n)), device_id_type=MESH
        )
    pl.semaphore_wait(barrier, n + 2)

    def windows(j, w):
        col = pl.ds(pl.multiple_of(j * PIECE, PIECE), PIECE)
        row = pl.ds(pl.multiple_of(w * hd, 32), hd)
        hrow = pl.ds(pl.multiple_of(j * PIECE + w * (PIECE // 2), 64), PIECE // 2)
        return (row, col), (row, col), (hrow, slice(None))

    def x_copy(j, a):
        win = windows(j, g)[a]
        return pltpu.make_async_remote_copy(
            src_ref=(gw_ref, uw_ref, dw_ref)[a].at[win],
            dst_ref=(far_g, far_u, far_d)[a].at[win],
            send_sem=xsend.at[j, a], recv_sem=xrecv.at[j, a],
            device_id=x_dev, device_id_type=MESH,
        )

    def y_copy(j, a, w):
        win = windows(j, w)[a]
        far = (far_g, far_u, far_d)[a].at[win]
        return pltpu.make_async_remote_copy(
            src_ref=far, dst_ref=far,
            send_sem=ysend.at[j, a], recv_sem=yrecv.at[j, a],
            device_id=y_dev, device_id_type=MESH,
        )

    def x_start(j):
        for a in range(3):
            x_copy(j, a).start()

    def forward(j):
        for a in range(3):
            x_copy(j, a).wait_recv()
            y_copy(j, a, g).start()

    def y_arrived(j):
        for a in range(3):
            y_copy(j, a, 1 - g).wait_recv()

    def z_copy(s, right):
        src = c - s if right else c + s
        blk = xt.at[:, rows_of(src, d), :]
        return pltpu.make_async_remote_copy(
            src_ref=acts_ref if s == 0 else blk, dst_ref=blk,
            send_sem=(rsend if right else lsend).at[s],
            recv_sem=(rrecv if right else lrecv).at[s],
            device_id=at(cc=c + 1 if right else c - 1), device_id_type=MESH,
        )

    def z_arrival(s, right):
        src = c - 1 - s if right else c + 1 + s
        blk = xt.at[:, rows_of(src, d), :]
        return pltpu.make_async_remote_copy(
            src_ref=blk, dst_ref=blk,
            send_sem=(rsend if right else lsend).at[s],
            recv_sem=(rrecv if right else lrecv).at[s],
            device_id=at(cc=c - 1 if right else c + 1), device_id_type=MESH,
        )

    def sib_copy(src, own=False, dd=d):
        blk = xt.at[:, rows_of(src, dd), :]
        return pltpu.make_async_remote_copy(
            src_ref=acts_ref if own else blk, dst_ref=blk,
            send_sem=ssend.at[src], recv_sem=srecv.at[src],
            device_id=sib, device_id_type=MESH,
        )

    def sends(s, right):
        return (c + 1 < n) & (c - s >= 0) if right else (c >= 1) & (c + s < n)

    def gets(s, right):
        return c - 1 - s >= 0 if right else c + 1 + s < n

    def z_start(s, right):
        @pl.when(sends(s, right))
        def _():
            z_copy(s, right).start()

    def z_got(s, right):
        @pl.when(gets(s, right))
        def _():
            z_arrival(s, right).wait_recv()

        if s + 1 < n - 1:
            z_start(s + 1, right)

        @pl.when(gets(s, right))
        def _():
            sib_copy(c - 1 - s if right else c + 1 + s).start()

    x_start(0)
    z_start(0, True)
    z_start(0, False)
    sib_copy(c, own=True).start()
    x_start(1)
    x_start(2)
    acc[...] = jnp.zeros_like(acc)

    lead = 2 * (n - 1)
    for j in range(lead):
        forward(j)
        if j + 3 < pieces:
            x_start(j + 3)
        if j % 2:
            z_got(j // 2, True)
            z_got(j // 2, False)

    for cp in own_copies:
        cp.wait()
    for src in range(n):
        sib_copy(src, dd=1 - d).wait_recv()

    blocks = half // 128
    for h in range(2):
        @pl.loop(0, blocks)
        def _(j):
            feat = pl.ds(pl.multiple_of(h * half + j * 128, 128), 128)
            lane = pl.ds(pl.multiple_of(j * 128, 128), 128)
            xs[h, :tokens, lane] = xt[0, feat, :].T
            xs[h, tokens:, lane] = xt[1, feat, :].T
            cot[h, :, lane] = xt[2, feat, :].T

    def compute(off, width):
        col = pl.ds(off, width)
        gates = nn(xs[r], own_g[:, col]) + nn(xs[1 - r], far_g[:, col])
        ups = nn(xs[r], own_u[:, col]) + nn(xs[1 - r], far_u[:, col])
        back = nt(cot[r], own_d[col, :]) + nt(cot[1 - r], far_d[col, :])
        pre_gate, tan_gate = gates[:tokens], gates[tokens:]
        pre_up, tan_up = ups[:tokens], ups[tokens:]
        slope, bend = slope_and_bend(pre_gate)
        gate_part = (back * (tan_up * slope + pre_up * bend * tan_gate)).astype(BF16)
        up_part = (back * slope * tan_gate).astype(BF16)
        for w_g, w_u, base in ((own_g, own_u, r), (far_g, far_u, 1 - r)):
            for q in range(0, half, part):
                rows = pl.ds(pl.multiple_of(base * half + q, 32), part)
                acc[rows, :] += nt(w_g[q:q + part, col], gate_part) + nt(
                    w_u[q:q + part, col], up_part
                )

    per = WIDE // PIECE
    steps = hidden // WIDE

    @pl.loop(0, steps)
    def _(i):
        for k in range(per):
            y_arrived(i * per + k)

        @pl.when(lead + i < pieces)
        def _():
            forward(lead + i)

        compute(pl.multiple_of(i * WIDE, WIDE), WIDE)

    for j in range(lead + steps, pieces):
        forward(j)
    for j in range(steps * per, pieces):
        y_arrived(j)
        compute(j * PIECE, PIECE)

    def q_copy(cc):
        return pltpu.make_async_remote_copy(
            src_ref=sib_out.at[cc], dst_ref=sib_in.at[cc],
            send_sem=qsend.at[cc], recv_sem=qrecv.at[cc],
            device_id=sib, device_id_type=MESH,
        )

    for cc in range(n):
        sib_out[cc] = acc[rows_of(cc, 1 - d), :].astype(BF16)
        q_copy(cc).start()

    def zr_copy(k):
        to = lax.rem(c + k, n)
        return pltpu.make_async_remote_copy(
            src_ref=z_out.at[k - 1], dst_ref=z_in.at[k - 1],
            send_sem=zsend.at[k - 1], recv_sem=zrecv.at[k - 1],
            device_id=at(cc=to), device_id_type=MESH,
        )

    for cc in range(n):
        q_copy(cc).wait_recv()
    for k in range(1, n):
        to = lax.rem(c + k, n)
        z_out[k - 1] = (acc[rows_of(to, d), :] + sib_in[to].astype(F32)).astype(BF16)
        zr_copy(k).start()
    total = acc[rows_of(c, d), :] + sib_in[c].astype(F32)
    for k in range(1, n):
        zr_copy(k).wait_recv()
        total = total + z_in[k - 1].astype(F32)
    out_ref[...] = total.astype(BF16)

    @pl.loop(0, pieces)
    def _(j):
        for a in range(3):
            x_copy(j, a).wait_send()
            y_copy(j, a, g).wait_send()

    for s in range(n - 1):
        for right in (True, False):
            @pl.when(sends(s, right))
            def _():
                z_copy(s, right).wait_send()
    for cc in range(n):
        sib_copy(cc).wait_send()
        q_copy(cc).wait_send()
    for k in range(1, n):
        zr_copy(k).wait_send()


def fused(n, inputs, probe, cotangent, gate_weight, up_weight, down_weight):
    tokens, part = inputs.shape
    half, hidden = gate_weight.shape
    wide = 2 * half
    pieces = hidden // PIECE
    acts = jnp.stack([inputs, probe, cotangent]).transpose(0, 2, 1)
    dma = pltpu.SemaphoreType.DMA
    any_spec = pl.BlockSpec(memory_space=pl.ANY)
    vmem = pltpu.VMEM
    out = pl.pallas_call(
        functools.partial(kernel, n),
        out_shape=jax.ShapeDtypeStruct((part, tokens), BF16),
        in_specs=[any_spec] * 4,
        out_specs=pl.BlockSpec(memory_space=pltpu.VMEM),
        scratch_shapes=[
            vmem((3, wide, tokens), BF16),
            vmem((2, 2 * tokens, half), BF16),
            vmem((2, tokens, half), BF16),
            vmem((half, hidden), BF16), vmem((half, hidden), BF16), vmem((hidden, half), BF16),
            vmem((half, hidden), BF16), vmem((half, hidden), BF16), vmem((hidden, half), BF16),
            vmem((wide, tokens), F32),
            vmem((n, part, tokens), BF16), vmem((n, part, tokens), BF16),
            vmem((n - 1, part, tokens), BF16), vmem((n - 1, part, tokens), BF16),
            dma((4,)),
            dma((pieces, 3)), dma((pieces, 3)), dma((pieces, 3)), dma((pieces, 3)),
            dma((n - 1,)), dma((n - 1,)), dma((n - 1,)), dma((n - 1,)),
            dma((n,)), dma((n,)), dma((n,)), dma((n,)),
            dma((n - 1,)), dma((n - 1,)),
        ],
        compiler_params=pltpu.CompilerParams(
            collective_id=0, has_side_effects=True, vmem_limit_bytes=60 * 2**20
        ),
        cost_estimate=pl.CostEstimate(
            flops=14 * tokens * wide * hidden,
            bytes_accessed=6 * half * hidden,
            transcendentals=tokens * hidden,
        ),
    )(acts, gate_weight, up_weight, down_weight)
    return out.T


def gathered(inputs, probe, cotangent, gate_weight, up_weight, down_weight):
    gate_full, up_full, down_full = (
        lax.all_gather(gate_weight, "row", axis=0, tiled=True),
        lax.all_gather(up_weight, "row", axis=0, tiled=True),
        lax.all_gather(down_weight, "row", axis=1, tiled=True),
    )
    in_piece = lax.all_gather(inputs, ("col", "depth"), axis=1, tiled=True)
    probe_piece = lax.all_gather(probe, ("col", "depth"), axis=1, tiled=True)
    cot_piece = lax.all_gather(cotangent, ("col", "depth"), axis=1, tiled=True)
    pre_gate, pre_up = nn(in_piece, gate_full), nn(in_piece, up_full)
    tan_gate, tan_up = nn(probe_piece, gate_full), nn(probe_piece, up_full)
    back = nt(cot_piece, down_full)
    slope = gelu_slope(pre_gate)
    gate_part = (back * (tan_up * slope + pre_up * gelu_bend(pre_gate) * tan_gate)).astype(BF16)
    up_part = (back * slope * tan_gate).astype(BF16)
    term = nt(gate_part, gate_full) + nt(up_part, up_full)
    return lax.psum_scatter(
        term.astype(BF16), ("col", "depth"), scatter_dimension=1, tiled=True
    )


def solution(mesh):
    sizes = dict(mesh.shape)
    n = sizes["col"]

    def per_device(*args):
        half, hidden = args[3].shape
        square = sizes["groups"] == 2 and sizes["row"] == 2 and sizes["depth"] == 2
        even = half % 128 == 0 and hidden % PIECE == 0 and args[0].shape[1] % 32 == 0
        small = 2 * (n - 1) <= hidden // PIECE and half * hidden <= 2**21
        if square and even and small:
            return fused(n, *args)
        return gathered(*args)

    in_specs = (
        P(("groups", "row"), ("col", "depth")),
        P(("groups", "row"), ("col", "depth")),
        P(("groups", "row"), ("col", "depth")),
        P("row", ("col", "depth")),
        P("row", ("col", "depth")),
        P(("col", "depth"), "row"),
    )
    out_specs = P(("groups", "row"), ("col", "depth"))
    return jax.shard_map(
        per_device, mesh=mesh, in_specs=in_specs, out_specs=out_specs, check_vma=False
    )
```

```python
import functools

import jax
import jax.numpy as jnp
from jax import lax
from jax.experimental import pallas as pl
from jax.experimental.pallas import tpu as pltpu
from jax.sharding import PartitionSpec as P

MESH = pl.DeviceIdType.MESH
F32, BF16 = jnp.float32, jnp.bfloat16
K0, K1 = 0.7978845608, 0.044715
PIECE = 128
WIDE = 256


def gelu_tanh(value):
    return 0.5 * value * (1.0 + jnp.tanh(K0 * (value + K1 * value * value * value)))


def gelu_slope(value):
    return jax.jvp(gelu_tanh, (value,), (jnp.ones_like(value),))[1]


def gelu_bend(value):
    return jax.jvp(gelu_slope, (value,), (jnp.ones_like(value),))[1]


def slope_and_bend(s):
    sq = s * s
    t = jnp.tanh(K0 * s * (1.0 + K1 * sq))
    du = K0 + (3.0 * K0 * K1) * sq
    e = 1.0 - t * t
    slope = 0.5 * (1.0 + t) + 0.5 * s * e * du
    bend = e * (K0 + (6.0 * K0 * K1) * sq - s * t * du * du)
    return slope, bend


def nt(a, b):
    return lax.dot_general(a, b, (((1,), (1,)), ((), ())), preferred_element_type=F32)


def nn(a, b):
    return jnp.dot(a, b, preferred_element_type=F32)


def kernel(
    n, in_ref, pr_ref, ct_ref, gw_ref, uw_ref, dw_ref, out_ref,
    raw, xt, xs, cot, own_g, own_u, own_d, far_g, far_u, far_d, acc,
    sib_out, sib_in, z_out, z_in,
    own_sem, xsend, xrecv, ysend, yrecv, rsend, rrecv, lsend, lrecv, ssend, srecv,
    qsend, qrecv, zsend, zrecv,
):
    g, r = lax.axis_index("groups"), lax.axis_index("row")
    c, d = lax.axis_index("col"), lax.axis_index("depth")
    half, hidden = gw_ref.shape
    tokens, part = in_ref.shape
    pieces = hidden // PIECE
    hd = half // 2

    def at(gg=g, rr=r, cc=c, dd=d):
        return (gg, rr, cc, dd)

    x_dev, y_dev, sib = at(rr=1 - r), at(gg=1 - g), at(dd=1 - d)

    def rows_of(cc, dd):
        return pl.ds(pl.multiple_of((cc * 2 + dd) * part, 32), part)

    own_copies = [
        pltpu.make_async_copy(gw_ref, own_g, own_sem.at[0]),
        pltpu.make_async_copy(uw_ref, own_u, own_sem.at[1]),
        pltpu.make_async_copy(dw_ref, own_d, own_sem.at[2]),
    ]
    raw_copies = [
        pltpu.make_async_copy(ref, raw.at[a], own_sem.at[3 + a])
        for a, ref in enumerate((in_ref, pr_ref, ct_ref))
    ]
    for cp in raw_copies:
        cp.start()

    barrier = pltpu.get_barrier_semaphore()
    for dev in (x_dev, y_dev, sib):
        pl.semaphore_signal(barrier, inc=1, device_id=dev, device_id_type=MESH)
    for k in range(1, n):
        pl.semaphore_signal(
            barrier, inc=1, device_id=at(cc=lax.rem(c + k, n)), device_id_type=MESH
        )
    pl.semaphore_wait(barrier, n + 2)

    def windows(j, w):
        col = pl.ds(pl.multiple_of(j * PIECE, PIECE), PIECE)
        row = pl.ds(pl.multiple_of(w * hd, 32), hd)
        hrow = pl.ds(pl.multiple_of(j * PIECE + w * (PIECE // 2), 64), PIECE // 2)
        return (row, col), (row, col), (hrow, slice(None))

    def x_copy(j, a):
        win = windows(j, g)[a]
        return pltpu.make_async_remote_copy(
            src_ref=(gw_ref, uw_ref, dw_ref)[a].at[win],
            dst_ref=(far_g, far_u, far_d)[a].at[win],
            send_sem=xsend.at[j, a], recv_sem=xrecv.at[j, a],
            device_id=x_dev, device_id_type=MESH,
        )

    def y_copy(j, a, w):
        win = windows(j, w)[a]
        far = (far_g, far_u, far_d)[a].at[win]
        return pltpu.make_async_remote_copy(
            src_ref=far, dst_ref=far,
            send_sem=ysend.at[j, a], recv_sem=yrecv.at[j, a],
            device_id=y_dev, device_id_type=MESH,
        )

    def x_start(j):
        for a in range(3):
            x_copy(j, a).start()

    def forward(j):
        for a in range(3):
            x_copy(j, a).wait_recv()
            y_copy(j, a, g).start()

    def y_arrived(j):
        for a in range(3):
            y_copy(j, a, 1 - g).wait_recv()

    def z_copy(s, right):
        src = c - s if right else c + s
        blk = xt.at[:, rows_of(src, d), :]
        return pltpu.make_async_remote_copy(
            src_ref=blk, dst_ref=blk,
            send_sem=(rsend if right else lsend).at[s],
            recv_sem=(rrecv if right else lrecv).at[s],
            device_id=at(cc=c + 1 if right else c - 1), device_id_type=MESH,
        )

    def z_arrival(s, right):
        src = c - 1 - s if right else c + 1 + s
        blk = xt.at[:, rows_of(src, d), :]
        return pltpu.make_async_remote_copy(
            src_ref=blk, dst_ref=blk,
            send_sem=(rsend if right else lsend).at[s],
            recv_sem=(rrecv if right else lrecv).at[s],
            device_id=at(cc=c - 1 if right else c + 1), device_id_type=MESH,
        )

    def sib_copy(src, dd=d):
        blk = xt.at[:, rows_of(src, dd), :]
        return pltpu.make_async_remote_copy(
            src_ref=blk, dst_ref=blk,
            send_sem=ssend.at[src], recv_sem=srecv.at[src],
            device_id=sib, device_id_type=MESH,
        )

    def sends(s, right):
        return (c + 1 < n) & (c - s >= 0) if right else (c >= 1) & (c + s < n)

    def gets(s, right):
        return c - 1 - s >= 0 if right else c + 1 + s < n

    def z_start(s, right):
        @pl.when(sends(s, right))
        def _():
            z_copy(s, right).start()

    def z_got(s, right):
        @pl.when(gets(s, right))
        def _():
            z_arrival(s, right).wait_recv()

        if s + 1 < n - 1:
            z_start(s + 1, right)

        @pl.when(gets(s, right))
        def _():
            sib_copy(c - 1 - s if right else c + 1 + s).start()

    for j in range(3):
        x_start(j)
    for a in range(3):
        raw_copies[a].wait()
        xt[a, rows_of(c, d), :] = raw[a].T
    z_start(0, True)
    z_start(0, False)
    sib_copy(c).start()
    for cp in own_copies:
        cp.start()
    acc[...] = jnp.zeros_like(acc)

    lead = 2 * (n - 1)
    for j in range(lead):
        forward(j)
        if j + 3 < pieces:
            x_start(j + 3)
        if j % 2:
            z_got(j // 2, True)
            z_got(j // 2, False)

    for cp in own_copies:
        cp.wait()
    for src in range(n):
        sib_copy(src, dd=1 - d).wait_recv()

    blocks = half // 128
    for h in range(2):
        @pl.loop(0, blocks)
        def _(j):
            feat = pl.ds(pl.multiple_of(h * half + j * 128, 128), 128)
            lane = pl.ds(pl.multiple_of(j * 128, 128), 128)
            xs[h, :tokens, lane] = xt[0, feat, :].T
            xs[h, tokens:, lane] = xt[1, feat, :].T
            cot[h, :, lane] = xt[2, feat, :].T

    def compute(off, width):
        col = pl.ds(off, width)
        gates = nn(xs[r], own_g[:, col]) + nn(xs[1 - r], far_g[:, col])
        ups = nn(xs[r], own_u[:, col]) + nn(xs[1 - r], far_u[:, col])
        back = nt(cot[r], own_d[col, :]) + nt(cot[1 - r], far_d[col, :])
        pre_gate, tan_gate = gates[:tokens], gates[tokens:]
        pre_up, tan_up = ups[:tokens], ups[tokens:]
        slope, bend = slope_and_bend(pre_gate)
        gate_part = (back * (tan_up * slope + pre_up * bend * tan_gate)).astype(BF16)
        up_part = (back * slope * tan_gate).astype(BF16)
        for w_g, w_u, base in ((own_g, own_u, r), (far_g, far_u, 1 - r)):
            for q in range(0, half, part):
                rows = pl.ds(pl.multiple_of(base * half + q, 32), part)
                acc[rows, :] += nt(w_g[q:q + part, col], gate_part) + nt(
                    w_u[q:q + part, col], up_part
                )

    per = WIDE // PIECE
    steps = hidden // WIDE

    @pl.loop(0, steps)
    def _(i):
        for k in range(per):
            y_arrived(i * per + k)

        compute(pl.multiple_of(i * WIDE, WIDE), WIDE)

        @pl.when(lead + i < pieces)
        def _():
            forward(lead + i)

    for j in range(lead + steps, pieces):
        forward(j)
    for j in range(steps * per, pieces):
        y_arrived(j)
        compute(j * PIECE, PIECE)

    def q_copy(cc):
        return pltpu.make_async_remote_copy(
            src_ref=sib_out.at[cc], dst_ref=sib_in.at[cc],
            send_sem=qsend.at[cc], recv_sem=qrecv.at[cc],
            device_id=sib, device_id_type=MESH,
        )

    side = (2 * c) // n

    def q_order(i):
        return (n - 1 - i) * (1 - side) + i * side

    for i in range(n):
        t = q_order(i)
        sib_out[t] = acc[rows_of(t, 1 - d), :].astype(BF16)
        q_copy(t).start()

    def z_sum(way, t):
        return pltpu.make_async_remote_copy(
            src_ref=z_out.at[t], dst_ref=z_in.at[way, t],
            send_sem=zsend.at[t], recv_sem=zrecv.at[way, t],
            device_id=at(cc=c + 1 - 2 * way), device_id_type=MESH,
        )

    def z_came(way, t):
        return pltpu.make_async_remote_copy(
            src_ref=z_out.at[t], dst_ref=z_in.at[way, t],
            send_sem=zsend.at[t], recv_sem=zrecv.at[way, t],
            device_id=at(cc=c - 1 + 2 * way), device_id_type=MESH,
        )

    def fed(way):
        return c * (1 - way) + (n - 1 - c) * way > 0

    def add_in(way, t):
        @pl.when(fed(way))
        def _():
            z_came(way, t).wait_recv()
            rows = rows_of(t, d)
            acc[rows, :] += z_in[way, t].astype(F32)

    def pass_on(way, t):
        @pl.when((t - c) * (1 - 2 * way) > 0)
        def _():
            add_in(way, t)
            z_out[t] = (acc[rows_of(t, d), :] + sib_in[t].astype(F32)).astype(BF16)
            z_sum(way, t).start()

    for i in range(n):
        t = q_order(i)
        q_copy(t).wait_recv()
        pass_on(side, t)
    for i in range(n - 1):
        pass_on(1 - side, n - 1 - q_order(i))
    add_in(side, c)
    add_in(1 - side, c)
    out_ref[...] = (acc[rows_of(c, d), :] + sib_in[c].astype(F32)).astype(BF16)

    @pl.loop(0, pieces)
    def _(j):
        for a in range(3):
            x_copy(j, a).wait_send()
            y_copy(j, a, g).wait_send()

    for s in range(n - 1):
        for right in (True, False):
            @pl.when(sends(s, right))
            def _():
                z_copy(s, right).wait_send()
    for cc in range(n):
        sib_copy(cc).wait_send()
        q_copy(cc).wait_send()
    for t in range(n):
        for way, away in ((0, t > c), (1, t < c)):
            @pl.when(away)
            def _():
                z_sum(way, t).wait_send()


def fused(n, inputs, probe, cotangent, gate_weight, up_weight, down_weight):
    tokens, part = inputs.shape
    half, hidden = gate_weight.shape
    wide = 2 * half
    pieces = hidden // PIECE
    dma = pltpu.SemaphoreType.DMA
    any_spec = pl.BlockSpec(memory_space=pl.ANY)
    vmem = pltpu.VMEM
    out = pl.pallas_call(
        functools.partial(kernel, n),
        out_shape=jax.ShapeDtypeStruct((part, tokens), BF16),
        in_specs=[any_spec] * 6,
        out_specs=pl.BlockSpec(memory_space=pltpu.VMEM),
        scratch_shapes=[
            vmem((3, tokens, part), BF16),
            vmem((3, wide, tokens), BF16),
            vmem((2, 2 * tokens, half), BF16),
            vmem((2, tokens, half), BF16),
            vmem((half, hidden), BF16), vmem((half, hidden), BF16), vmem((hidden, half), BF16),
            vmem((half, hidden), BF16), vmem((half, hidden), BF16), vmem((hidden, half), BF16),
            vmem((wide, tokens), F32),
            vmem((n, part, tokens), BF16), vmem((n, part, tokens), BF16),
            vmem((n, part, tokens), BF16), vmem((2, n, part, tokens), BF16),
            dma((6,)),
            dma((pieces, 3)), dma((pieces, 3)), dma((pieces, 3)), dma((pieces, 3)),
            dma((n - 1,)), dma((n - 1,)), dma((n - 1,)), dma((n - 1,)),
            dma((n,)), dma((n,)), dma((n,)), dma((n,)),
            dma((n,)), dma((2, n)),
        ],
        compiler_params=pltpu.CompilerParams(
            collective_id=0, has_side_effects=True, vmem_limit_bytes=60 * 2**20
        ),
        cost_estimate=pl.CostEstimate(
            flops=14 * tokens * wide * hidden,
            bytes_accessed=6 * half * hidden,
            transcendentals=tokens * hidden,
        ),
    )(inputs, probe, cotangent, gate_weight, up_weight, down_weight)
    return out.T


def gathered(inputs, probe, cotangent, gate_weight, up_weight, down_weight):
    gate_full, up_full, down_full = (
        lax.all_gather(gate_weight, "row", axis=0, tiled=True),
        lax.all_gather(up_weight, "row", axis=0, tiled=True),
        lax.all_gather(down_weight, "row", axis=1, tiled=True),
    )
    in_piece = lax.all_gather(inputs, ("col", "depth"), axis=1, tiled=True)
    probe_piece = lax.all_gather(probe, ("col", "depth"), axis=1, tiled=True)
    cot_piece = lax.all_gather(cotangent, ("col", "depth"), axis=1, tiled=True)
    pre_gate, pre_up = nn(in_piece, gate_full), nn(in_piece, up_full)
    tan_gate, tan_up = nn(probe_piece, gate_full), nn(probe_piece, up_full)
    back = nt(cot_piece, down_full)
    slope = gelu_slope(pre_gate)
    gate_part = (back * (tan_up * slope + pre_up * gelu_bend(pre_gate) * tan_gate)).astype(BF16)
    up_part = (back * slope * tan_gate).astype(BF16)
    term = nt(gate_part, gate_full) + nt(up_part, up_full)
    return lax.psum_scatter(
        term.astype(BF16), ("col", "depth"), scatter_dimension=1, tiled=True
    )


def solution(mesh):
    sizes = dict(mesh.shape)
    n = sizes["col"]

    def per_device(*args):
        half, hidden = args[3].shape
        square = sizes["groups"] == 2 and sizes["row"] == 2 and sizes["depth"] == 2
        even = half % 128 == 0 and hidden % PIECE == 0 and args[0].shape[1] % 32 == 0
        small = 2 * (n - 1) <= hidden // PIECE and half * hidden <= 2**21
        if square and even and small:
            return fused(n, *args)
        return gathered(*args)

    in_specs = (
        P(("groups", "row"), ("col", "depth")),
        P(("groups", "row"), ("col", "depth")),
        P(("groups", "row"), ("col", "depth")),
        P("row", ("col", "depth")),
        P("row", ("col", "depth")),
        P(("col", "depth"), "row"),
    )
    out_specs = P(("groups", "row"), ("col", "depth"))
    return jax.shard_map(
        per_device, mesh=mesh, in_specs=in_specs, out_specs=out_specs, check_vma=False
    )
```

```python
import functools

import jax
import jax.numpy as jnp
from jax import lax
from jax.experimental import pallas as pl
from jax.experimental.pallas import tpu as pltpu
from jax.sharding import PartitionSpec as P

MESH = pl.DeviceIdType.MESH
F32, BF16 = jnp.float32, jnp.bfloat16
K0, K1 = 0.7978845608, 0.044715
PIECE = 128
WIDE = 256


def gelu_tanh(value):
    return 0.5 * value * (1.0 + jnp.tanh(K0 * (value + K1 * value * value * value)))


def gelu_slope(value):
    return jax.jvp(gelu_tanh, (value,), (jnp.ones_like(value),))[1]


def gelu_bend(value):
    return jax.jvp(gelu_slope, (value,), (jnp.ones_like(value),))[1]


def slope_and_bend(s):
    sq = s * s
    t = jnp.tanh(K0 * s * (1.0 + K1 * sq))
    du = K0 + (3.0 * K0 * K1) * sq
    e = 1.0 - t * t
    slope = 0.5 * (1.0 + t) + 0.5 * s * e * du
    bend = e * (K0 + (6.0 * K0 * K1) * sq - s * t * du * du)
    return slope, bend


def nt(a, b):
    return lax.dot_general(a, b, (((1,), (1,)), ((), ())), preferred_element_type=F32)


def nn(a, b):
    return jnp.dot(a, b, preferred_element_type=F32)


def kernel(
    n, in_ref, pr_ref, ct_ref, gw_ref, uw_ref, dw_ref, out_ref,
    xt, xs, cot, own_g, own_u, own_d, far_g, far_u, far_d, acc,
    sib_out, sib_in, z_out, z_in,
    own_sem, xsend, xrecv, ysend, yrecv, rsend, rrecv, lsend, lrecv, ssend, srecv,
    qsend, qrecv, zsend, zrecv,
):
    g, r = lax.axis_index("groups"), lax.axis_index("row")
    c, d = lax.axis_index("col"), lax.axis_index("depth")
    half, hidden = gw_ref.shape
    part, tokens = in_ref.shape
    pieces = hidden // PIECE
    hd = half // 2

    def at(gg=g, rr=r, cc=c, dd=d):
        return (gg, rr, cc, dd)

    x_dev, y_dev, sib = at(rr=1 - r), at(gg=1 - g), at(dd=1 - d)

    def rows_of(cc, dd):
        return pl.ds(pl.multiple_of((cc * 2 + dd) * part, 32), part)

    own_copies = [
        pltpu.make_async_copy(gw_ref, own_g, own_sem.at[0]),
        pltpu.make_async_copy(uw_ref, own_u, own_sem.at[1]),
        pltpu.make_async_copy(dw_ref, own_d, own_sem.at[2]),
    ]
    raw_copies = [
        pltpu.make_async_copy(ref, xt.at[a, rows_of(c, d), :], own_sem.at[3 + a])
        for a, ref in enumerate((in_ref, pr_ref, ct_ref))
    ]
    for cp in raw_copies:
        cp.start()

    barrier = pltpu.get_barrier_semaphore()
    for dev in (x_dev, y_dev, sib):
        pl.semaphore_signal(barrier, inc=1, device_id=dev, device_id_type=MESH)
    for k in range(1, n):
        pl.semaphore_signal(
            barrier, inc=1, device_id=at(cc=lax.rem(c + k, n)), device_id_type=MESH
        )
    pl.semaphore_wait(barrier, n + 2)

    def windows(j, w):
        col = pl.ds(pl.multiple_of(j * PIECE, PIECE), PIECE)
        row = pl.ds(pl.multiple_of(w * hd, 32), hd)
        hrow = pl.ds(pl.multiple_of(j * PIECE + w * (PIECE // 2), 64), PIECE // 2)
        return (row, col), (row, col), (hrow, slice(None))

    def x_copy(j, a):
        win = windows(j, g)[a]
        return pltpu.make_async_remote_copy(
            src_ref=(gw_ref, uw_ref, dw_ref)[a].at[win],
            dst_ref=(far_g, far_u, far_d)[a].at[win],
            send_sem=xsend.at[j, a], recv_sem=xrecv.at[j, a],
            device_id=x_dev, device_id_type=MESH,
        )

    def y_copy(j, a, w):
        win = windows(j, w)[a]
        far = (far_g, far_u, far_d)[a].at[win]
        return pltpu.make_async_remote_copy(
            src_ref=far, dst_ref=far,
            send_sem=ysend.at[j, a], recv_sem=yrecv.at[j, a],
            device_id=y_dev, device_id_type=MESH,
        )

    def x_start(j):
        for a in range(3):
            x_copy(j, a).start()

    def forward(j):
        for a in range(3):
            x_copy(j, a).wait_recv()
            y_copy(j, a, g).start()

    def forward_next(q):
        for a in range(3):
            @pl.when((q % 3 == a) & (q < 3 * pieces))
            def _():
                x_copy(q // 3, a).wait_recv()
                y_copy(q // 3, a, g).start()

    def y_arrived(j):
        for a in range(3):
            y_copy(j, a, 1 - g).wait_recv()

    def z_copy(s, right):
        src = c - s if right else c + s
        blk = xt.at[:, rows_of(src, d), :]
        return pltpu.make_async_remote_copy(
            src_ref=blk, dst_ref=blk,
            send_sem=(rsend if right else lsend).at[s],
            recv_sem=(rrecv if right else lrecv).at[s],
            device_id=at(cc=c + 1 if right else c - 1), device_id_type=MESH,
        )

    def z_arrival(s, right):
        src = c - 1 - s if right else c + 1 + s
        blk = xt.at[:, rows_of(src, d), :]
        return pltpu.make_async_remote_copy(
            src_ref=blk, dst_ref=blk,
            send_sem=(rsend if right else lsend).at[s],
            recv_sem=(rrecv if right else lrecv).at[s],
            device_id=at(cc=c - 1 if right else c + 1), device_id_type=MESH,
        )

    def sib_copy(src, dd=d):
        blk = xt.at[:, rows_of(src, dd), :]
        return pltpu.make_async_remote_copy(
            src_ref=blk, dst_ref=blk,
            send_sem=ssend.at[src], recv_sem=srecv.at[src],
            device_id=sib, device_id_type=MESH,
        )

    def sends(s, right):
        return (c + 1 < n) & (c - s >= 0) if right else (c >= 1) & (c + s < n)

    def gets(s, right):
        return c - 1 - s >= 0 if right else c + 1 + s < n

    def z_start(s, right):
        @pl.when(sends(s, right))
        def _():
            z_copy(s, right).start()

    def z_got(s, right):
        @pl.when(gets(s, right))
        def _():
            z_arrival(s, right).wait_recv()

        if s + 1 < n - 1:
            z_start(s + 1, right)

        @pl.when(gets(s, right))
        def _():
            sib_copy(c - 1 - s if right else c + 1 + s).start()

    for j in range(3):
        x_start(j)
    for a in range(3):
        raw_copies[a].wait()
    z_start(0, True)
    z_start(0, False)
    sib_copy(c).start()
    for cp in own_copies:
        cp.start()
    acc[...] = jnp.zeros_like(acc)

    blocks = half // 128

    def token_major(h):
        for src in range(n // 2):
            sib_copy(h * (n // 2) + src, dd=1 - d).wait_recv()

        @pl.loop(0, blocks)
        def _(j):
            feat = pl.ds(pl.multiple_of(h * half + j * 128, 128), 128)
            lane = pl.ds(pl.multiple_of(j * 128, 128), 128)
            xs[h, :tokens, lane] = xt[0, feat, :].T
            xs[h, tokens:, lane] = xt[1, feat, :].T
            cot[h, :, lane] = xt[2, feat, :].T

    side = (2 * c) // n
    near = n // 2 - 1
    lead = 2 * (n - 1)
    for j in range(lead):
        forward(j)
        if j + 3 < pieces:
            x_start(j + 3)
        if j % 2:
            z_got(j // 2, True)
            z_got(j // 2, False)
        if j == 2 * near:
            token_major(side)
    for cp in own_copies:
        cp.wait()
    token_major(1 - side)

    def forward_half(off, width, last=None):
        col = pl.ds(off, width)
        gates, ups = nn(xs[r], own_g[:, col]), nn(xs[r], own_u[:, col])
        back = nt(cot[r], own_d[col, :])
        if last is not None:
            y_copy(last, 0, 1 - g).wait_recv()
        gates = gates + nn(xs[1 - r], far_g[:, col])
        if last is not None:
            y_copy(last, 1, 1 - g).wait_recv()
        ups = ups + nn(xs[1 - r], far_u[:, col])
        if last is not None:
            y_copy(last, 2, 1 - g).wait_recv()
        back = back + nt(cot[1 - r], far_d[col, :])
        pre_gate, tan_gate = gates[:tokens], gates[tokens:]
        pre_up, tan_up = ups[:tokens], ups[tokens:]
        slope, bend = slope_and_bend(pre_gate)
        gate_part = (back * (tan_up * slope + pre_up * bend * tan_gate)).astype(BF16)
        up_part = (back * slope * tan_gate).astype(BF16)
        return gate_part, up_part

    def backward_half(off, width, gate_part, up_part):
        col = pl.ds(off, width)
        for w_g, w_u, base in ((own_g, own_u, r), (far_g, far_u, 1 - r)):
            for q in range(0, half, part):
                rows = pl.ds(pl.multiple_of(base * half + q, 32), part)
                acc[rows, :] += nt(w_g[q:q + part, col], gate_part) + nt(
                    w_u[q:q + part, col], up_part
                )

    per = WIDE // PIECE
    steps = hidden // WIDE

    begin = 3 * lead + 2
    forward_next(begin - 2)
    forward_next(begin - 1)

    @pl.loop(0, steps)
    def _(i):
        for k in range(per):
            y_arrived(i * per + k)
        off = pl.multiple_of(i * WIDE, WIDE)
        parts = forward_half(off, WIDE)
        forward_next(begin + 2 * i)
        backward_half(off, WIDE, *parts)
        forward_next(begin + 2 * i + 1)

    for q in range(begin + 2 * steps, 3 * pieces):
        forward_next(q)
    for j in range(steps * per, pieces):
        off = j * PIECE
        backward_half(off, PIECE, *forward_half(off, PIECE, j))

    def q_copy(cc):
        return pltpu.make_async_remote_copy(
            src_ref=sib_out.at[cc], dst_ref=sib_in.at[cc],
            send_sem=qsend.at[cc], recv_sem=qrecv.at[cc],
            device_id=sib, device_id_type=MESH,
        )

    def q_order(i):
        return (n - 1 - i) * (1 - side) + i * side

    for i in range(n):
        t = q_order(i)
        sib_out[t] = acc[rows_of(t, 1 - d), :].astype(BF16)
        q_copy(t).start()

    def z_sum(way, t):
        return pltpu.make_async_remote_copy(
            src_ref=z_out.at[t], dst_ref=z_in.at[way, t],
            send_sem=zsend.at[t], recv_sem=zrecv.at[way, t],
            device_id=at(cc=c + 1 - 2 * way), device_id_type=MESH,
        )

    def z_came(way, t):
        return pltpu.make_async_remote_copy(
            src_ref=z_out.at[t], dst_ref=z_in.at[way, t],
            send_sem=zsend.at[t], recv_sem=zrecv.at[way, t],
            device_id=at(cc=c - 1 + 2 * way), device_id_type=MESH,
        )

    def fed(way):
        return c * (1 - way) + (n - 1 - c) * way > 0

    def add_in(way, t):
        @pl.when(fed(way))
        def _():
            z_came(way, t).wait_recv()
            rows = rows_of(t, d)
            acc[rows, :] += z_in[way, t].astype(F32)

    def pass_on(way, t):
        @pl.when((t - c) * (1 - 2 * way) > 0)
        def _():
            add_in(way, t)
            z_out[t] = (acc[rows_of(t, d), :] + sib_in[t].astype(F32)).astype(BF16)
            z_sum(way, t).start()

    for i in range(n):
        t = q_order(i)
        q_copy(t).wait_recv()
        pass_on(side, t)
    for i in range(n - 1):
        pass_on(1 - side, n - 1 - q_order(i))
    add_in(side, c)
    add_in(1 - side, c)
    out_ref[...] = (acc[rows_of(c, d), :] + sib_in[c].astype(F32)).astype(BF16)

    @pl.loop(0, pieces)
    def _(j):
        for a in range(3):
            x_copy(j, a).wait_send()
            y_copy(j, a, g).wait_send()

    for s in range(n - 1):
        for right in (True, False):
            @pl.when(sends(s, right))
            def _():
                z_copy(s, right).wait_send()
    for cc in range(n):
        sib_copy(cc).wait_send()
        q_copy(cc).wait_send()
    for t in range(n):
        for way, away in ((0, t > c), (1, t < c)):
            @pl.when(away)
            def _():
                z_sum(way, t).wait_send()


def fused(n, inputs, probe, cotangent, gate_weight, up_weight, down_weight):
    tokens, part = inputs.shape
    half, hidden = gate_weight.shape
    wide = 2 * half
    pieces = hidden // PIECE
    dma = pltpu.SemaphoreType.DMA
    any_spec = pl.BlockSpec(memory_space=pl.ANY)
    vmem = pltpu.VMEM
    out = pl.pallas_call(
        functools.partial(kernel, n),
        out_shape=jax.ShapeDtypeStruct((part, tokens), BF16),
        in_specs=[any_spec] * 6,
        out_specs=pl.BlockSpec(memory_space=pltpu.VMEM),
        scratch_shapes=[
            vmem((3, wide, tokens), BF16),
            vmem((2, 2 * tokens, half), BF16),
            vmem((2, tokens, half), BF16),
            vmem((half, hidden), BF16), vmem((half, hidden), BF16), vmem((hidden, half), BF16),
            vmem((half, hidden), BF16), vmem((half, hidden), BF16), vmem((hidden, half), BF16),
            vmem((wide, tokens), F32),
            vmem((n, part, tokens), BF16), vmem((n, part, tokens), BF16),
            vmem((n, part, tokens), BF16), vmem((2, n, part, tokens), BF16),
            dma((6,)),
            dma((pieces, 3)), dma((pieces, 3)), dma((pieces, 3)), dma((pieces, 3)),
            dma((n - 1,)), dma((n - 1,)), dma((n - 1,)), dma((n - 1,)),
            dma((n,)), dma((n,)), dma((n,)), dma((n,)),
            dma((n,)), dma((2, n)),
        ],
        compiler_params=pltpu.CompilerParams(
            collective_id=0, has_side_effects=True, vmem_limit_bytes=60 * 2**20
        ),
        cost_estimate=pl.CostEstimate(
            flops=14 * tokens * wide * hidden,
            bytes_accessed=6 * half * hidden,
            transcendentals=tokens * hidden,
        ),
    )(inputs.T, probe.T, cotangent.T, gate_weight, up_weight, down_weight)
    return out.T


def gathered(inputs, probe, cotangent, gate_weight, up_weight, down_weight):
    gate_full, up_full, down_full = (
        lax.all_gather(gate_weight, "row", axis=0, tiled=True),
        lax.all_gather(up_weight, "row", axis=0, tiled=True),
        lax.all_gather(down_weight, "row", axis=1, tiled=True),
    )
    in_piece = lax.all_gather(inputs, ("col", "depth"), axis=1, tiled=True)
    probe_piece = lax.all_gather(probe, ("col", "depth"), axis=1, tiled=True)
    cot_piece = lax.all_gather(cotangent, ("col", "depth"), axis=1, tiled=True)
    pre_gate, pre_up = nn(in_piece, gate_full), nn(in_piece, up_full)
    tan_gate, tan_up = nn(probe_piece, gate_full), nn(probe_piece, up_full)
    back = nt(cot_piece, down_full)
    slope = gelu_slope(pre_gate)
    gate_part = (back * (tan_up * slope + pre_up * gelu_bend(pre_gate) * tan_gate)).astype(BF16)
    up_part = (back * slope * tan_gate).astype(BF16)
    term = nt(gate_part, gate_full) + nt(up_part, up_full)
    return lax.psum_scatter(
        term.astype(BF16), ("col", "depth"), scatter_dimension=1, tiled=True
    )


def solution(mesh):
    sizes = dict(mesh.shape)
    n = sizes["col"]

    def per_device(*args):
        half, hidden = args[3].shape
        square = sizes["groups"] == 2 and sizes["row"] == 2 and sizes["depth"] == 2
        even = half % 128 == 0 and hidden % PIECE == 0 and args[0].shape[1] % 32 == 0
        small = 2 * (n - 1) <= hidden // PIECE and half * hidden <= 2**21
        if square and even and small:
            return fused(n, *args)
        return gathered(*args)

    in_specs = (
        P(("groups", "row"), ("col", "depth")),
        P(("groups", "row"), ("col", "depth")),
        P(("groups", "row"), ("col", "depth")),
        P("row", ("col", "depth")),
        P("row", ("col", "depth")),
        P(("col", "depth"), "row"),
    )
    out_specs = P(("groups", "row"), ("col", "depth"))
    return jax.shard_map(
        per_device, mesh=mesh, in_specs=in_specs, out_specs=out_specs, check_vma=False
    )
```

```python
import functools

import jax
import jax.numpy as jnp
from jax import lax
from jax.experimental import pallas as pl
from jax.experimental.pallas import tpu as pltpu
from jax.sharding import PartitionSpec as P

MESH = pl.DeviceIdType.MESH
F32, BF16 = jnp.float32, jnp.bfloat16
K0, K1 = 0.7978845608, 0.044715
PIECE = 128
WIDE = 256


def gelu_tanh(value):
    return 0.5 * value * (1.0 + jnp.tanh(K0 * (value + K1 * value * value * value)))


def gelu_slope(value):
    return jax.jvp(gelu_tanh, (value,), (jnp.ones_like(value),))[1]


def gelu_bend(value):
    return jax.jvp(gelu_slope, (value,), (jnp.ones_like(value),))[1]


def slope_and_bend(s):
    sq = s * s
    t = jnp.tanh(K0 * s * (1.0 + K1 * sq))
    du = K0 + (3.0 * K0 * K1) * sq
    e = 1.0 - t * t
    slope = 0.5 * (1.0 + t) + 0.5 * s * e * du
    bend = e * (K0 + (6.0 * K0 * K1) * sq - s * t * du * du)
    return slope, bend


def nt(a, b):
    return lax.dot_general(a, b, (((1,), (1,)), ((), ())), preferred_element_type=F32)


def nn(a, b):
    return jnp.dot(a, b, preferred_element_type=F32)


def kernel(
    n, in_ref, pr_ref, ct_ref, gw_ref, uw_ref, dw_ref, out_ref,
    xt, xs, cot, own_g, own_u, own_d, far_g, far_u, far_d, acc,
    sib_out, sib_in, z_out, z_in,
    own_sem, xsend, xrecv, ysend, yrecv, rsend, rrecv, lsend, lrecv, ssend, srecv,
    qsend, qrecv, zsend, zrecv,
):
    g, r = lax.axis_index("groups"), lax.axis_index("row")
    c, d = lax.axis_index("col"), lax.axis_index("depth")
    half, hidden = gw_ref.shape
    part, tokens = in_ref.shape
    pieces = hidden // PIECE
    hd = half // 2

    def at(gg=g, rr=r, cc=c, dd=d):
        return (gg, rr, cc, dd)

    x_dev, y_dev, sib = at(rr=1 - r), at(gg=1 - g), at(dd=1 - d)

    def rows_of(cc, dd):
        return pl.ds(pl.multiple_of((cc * 2 + dd) * part, 32), part)

    own_copies = [
        pltpu.make_async_copy(gw_ref, own_g, own_sem.at[0]),
        pltpu.make_async_copy(uw_ref, own_u, own_sem.at[1]),
        pltpu.make_async_copy(dw_ref, own_d, own_sem.at[2]),
    ]
    raw_copies = [
        pltpu.make_async_copy(ref, xt.at[a, rows_of(c, d), :], own_sem.at[3 + a])
        for a, ref in enumerate((in_ref, pr_ref, ct_ref))
    ]
    for cp in raw_copies:
        cp.start()

    barrier = pltpu.get_barrier_semaphore()
    for dev in (x_dev, y_dev, sib):
        pl.semaphore_signal(barrier, inc=1, device_id=dev, device_id_type=MESH)
    for k in range(1, n):
        pl.semaphore_signal(
            barrier, inc=1, device_id=at(cc=lax.rem(c + k, n)), device_id_type=MESH
        )
    pl.semaphore_wait(barrier, n + 2)

    def windows(j, w):
        col = pl.ds(pl.multiple_of(j * PIECE, PIECE), PIECE)
        row = pl.ds(pl.multiple_of(w * hd, 32), hd)
        quarter = PIECE // 4
        first = pl.multiple_of(j * PIECE + w * (PIECE // 2), 64)
        second = pl.multiple_of(j * PIECE + w * (PIECE // 2) + quarter, 32)
        low, high = pl.ds(first, quarter), pl.ds(second, quarter)
        return (row, col), (row, col), (low, slice(None)), (high, slice(None))

    def x_copy(j, a):
        win = windows(j, g)[a]
        return pltpu.make_async_remote_copy(
            src_ref=(gw_ref, uw_ref, dw_ref, dw_ref)[a].at[win],
            dst_ref=(far_g, far_u, far_d, far_d)[a].at[win],
            send_sem=xsend.at[j, a], recv_sem=xrecv.at[j, a],
            device_id=x_dev, device_id_type=MESH,
        )

    def y_copy(j, a, w):
        win = windows(j, w)[a]
        far = (far_g, far_u, far_d, far_d)[a].at[win]
        return pltpu.make_async_remote_copy(
            src_ref=far, dst_ref=far,
            send_sem=ysend.at[j, a], recv_sem=yrecv.at[j, a],
            device_id=y_dev, device_id_type=MESH,
        )

    def x_start(j):
        for a in range(4):
            x_copy(j, a).start()

    def forward(j):
        for a in range(4):
            x_copy(j, a).wait_recv()
            y_copy(j, a, g).start()

    def forward_next(q):
        for a in range(4):
            @pl.when((q % 4 == a) & (q < 4 * pieces))
            def _():
                x_copy(q // 4, a).wait_recv()
                y_copy(q // 4, a, g).start()

    def y_arrived(j):
        for a in range(4):
            y_copy(j, a, 1 - g).wait_recv()

    def z_copy(s, right):
        src = c - s if right else c + s
        blk = xt.at[:, rows_of(src, d), :]
        return pltpu.make_async_remote_copy(
            src_ref=blk, dst_ref=blk,
            send_sem=(rsend if right else lsend).at[s],
            recv_sem=(rrecv if right else lrecv).at[s],
            device_id=at(cc=c + 1 if right else c - 1), device_id_type=MESH,
        )

    def z_arrival(s, right):
        src = c - 1 - s if right else c + 1 + s
        blk = xt.at[:, rows_of(src, d), :]
        return pltpu.make_async_remote_copy(
            src_ref=blk, dst_ref=blk,
            send_sem=(rsend if right else lsend).at[s],
            recv_sem=(rrecv if right else lrecv).at[s],
            device_id=at(cc=c - 1 if right else c + 1), device_id_type=MESH,
        )

    def sib_copy(src, dd=d):
        blk = xt.at[:, rows_of(src, dd), :]
        return pltpu.make_async_remote_copy(
            src_ref=blk, dst_ref=blk,
            send_sem=ssend.at[src], recv_sem=srecv.at[src],
            device_id=sib, device_id_type=MESH,
        )

    def sends(s, right):
        return (c + 1 < n) & (c - s >= 0) if right else (c >= 1) & (c + s < n)

    def gets(s, right):
        return c - 1 - s >= 0 if right else c + 1 + s < n

    def z_start(s, right):
        @pl.when(sends(s, right))
        def _():
            z_copy(s, right).start()

    def z_got(s, right):
        @pl.when(gets(s, right))
        def _():
            z_arrival(s, right).wait_recv()

        if s + 1 < n - 1:
            z_start(s + 1, right)

        @pl.when(gets(s, right))
        def _():
            sib_copy(c - 1 - s if right else c + 1 + s).start()

    for j in range(3):
        x_start(j)
    for a in range(3):
        raw_copies[a].wait()
    z_start(0, True)
    z_start(0, False)
    sib_copy(c).start()
    for cp in own_copies:
        cp.start()
    acc[...] = jnp.zeros_like(acc)

    blocks = half // 128

    def token_major(h):
        for src in range(n // 2):
            sib_copy(h * (n // 2) + src, dd=1 - d).wait_recv()

        @pl.loop(0, blocks)
        def _(j):
            feat = pl.ds(pl.multiple_of(h * half + j * 128, 128), 128)
            lane = pl.ds(pl.multiple_of(j * 128, 128), 128)
            xs[h, :tokens, lane] = xt[0, feat, :].T
            xs[h, tokens:, lane] = xt[1, feat, :].T
            cot[h, :, lane] = xt[2, feat, :].T

    side = (2 * c) // n
    near = n // 2 - 1
    lead = 2 * (n - 1)
    for j in range(lead):
        forward(j)
        if j + 3 < pieces:
            x_start(j + 3)
        if j % 2:
            z_got(j // 2, True)
            z_got(j // 2, False)
        if j == 2 * near:
            token_major(side)
    for cp in own_copies:
        cp.wait()
    token_major(1 - side)

    def forward_half(off, width, last=None):
        col = pl.ds(off, width)
        gates, ups = nn(xs[r], own_g[:, col]), nn(xs[r], own_u[:, col])
        back = nt(cot[r], own_d[col, :])
        if last is not None:
            y_copy(last, 0, 1 - g).wait_recv()
        gates = gates + nn(xs[1 - r], far_g[:, col])
        if last is not None:
            y_copy(last, 1, 1 - g).wait_recv()
        ups = ups + nn(xs[1 - r], far_u[:, col])
        if last is not None:
            y_copy(last, 2, 1 - g).wait_recv()
            y_copy(last, 3, 1 - g).wait_recv()
        back = back + nt(cot[1 - r], far_d[col, :])
        pre_gate, tan_gate = gates[:tokens], gates[tokens:]
        pre_up, tan_up = ups[:tokens], ups[tokens:]
        slope, bend = slope_and_bend(pre_gate)
        gate_part = (back * (tan_up * slope + pre_up * bend * tan_gate)).astype(BF16)
        up_part = (back * slope * tan_gate).astype(BF16)
        return gate_part, up_part

    def backward_half(off, width, gate_part, up_part):
        col = pl.ds(off, width)
        for w_g, w_u, base in ((own_g, own_u, r), (far_g, far_u, 1 - r)):
            for q in range(0, half, part):
                rows = pl.ds(pl.multiple_of(base * half + q, 32), part)
                acc[rows, :] += nt(w_g[q:q + part, col], gate_part) + nt(
                    w_u[q:q + part, col], up_part
                )

    per = WIDE // PIECE
    steps = hidden // WIDE

    begin = 4 * lead + 1
    forward_next(begin - 1)

    @pl.loop(0, steps)
    def _(i):
        for k in range(per):
            y_arrived(i * per + k)
        off = pl.multiple_of(i * WIDE, WIDE)
        parts = forward_half(off, WIDE)
        forward_next(begin + 3 * i)
        forward_next(begin + 3 * i + 1)
        backward_half(off, WIDE, *parts)
        forward_next(begin + 3 * i + 2)

    for q in range(begin + 3 * steps, 4 * pieces):
        forward_next(q)
    for j in range(steps * per, pieces):
        off = j * PIECE
        backward_half(off, PIECE, *forward_half(off, PIECE, j))

    def q_copy(cc):
        return pltpu.make_async_remote_copy(
            src_ref=sib_out.at[cc], dst_ref=sib_in.at[cc],
            send_sem=qsend.at[cc], recv_sem=qrecv.at[cc],
            device_id=sib, device_id_type=MESH,
        )

    def q_order(i):
        return (n - 1 - i) * (1 - side) + i * side

    for i in range(n):
        t = q_order(i)
        sib_out[t] = acc[rows_of(t, 1 - d), :].astype(BF16)
        q_copy(t).start()

    cut = part // 2

    def z_sum(way, t, h, back=False):
        rows = pl.ds(h * cut, cut)
        step = 1 - 2 * way
        return pltpu.make_async_remote_copy(
            src_ref=z_out.at[t, rows], dst_ref=z_in.at[way, t, rows],
            send_sem=zsend.at[t, h], recv_sem=zrecv.at[way, t, h],
            device_id=at(cc=c - step if back else c + step), device_id_type=MESH,
        )

    def shard(t, h):
        return pl.ds(pl.multiple_of((t * 2 + d) * part + h * cut, 16), cut)

    def add_in(way, t, h):
        @pl.when(c * (1 - way) + (n - 1 - c) * way > 0)
        def _():
            z_sum(way, t, h, back=True).wait_recv()
            acc[shard(t, h), :] += z_in[way, t, h * cut:(h + 1) * cut].astype(F32)

    def with_pair(t, h):
        other = sib_in[t, h * cut:(h + 1) * cut].astype(F32)
        return (acc[shard(t, h), :] + other).astype(BF16)

    def pass_on(way, t):
        @pl.when((t - c) * (1 - 2 * way) > 0)
        def _():
            for h in range(2):
                add_in(way, t, h)
                z_out[t, h * cut:(h + 1) * cut] = with_pair(t, h)
                z_sum(way, t, h).start()

    for i in range(n - 1):
        if i == 0:
            q_copy(q_order(0)).wait_recv()
        pass_on(side, q_order(i))
        if i == 0:
            for k in range(1, n):
                q_copy(q_order(k)).wait_recv()
        pass_on(1 - side, q_order(n - 1 - i))
    for h in range(2):
        add_in(side, c, h)
        add_in(1 - side, c, h)
        out_ref[h * cut:(h + 1) * cut, :] = with_pair(c, h)

    @pl.loop(0, pieces)
    def _(j):
        for a in range(4):
            x_copy(j, a).wait_send()
            y_copy(j, a, g).wait_send()

    for s in range(n - 1):
        for right in (True, False):
            @pl.when(sends(s, right))
            def _():
                z_copy(s, right).wait_send()
    for cc in range(n):
        sib_copy(cc).wait_send()
        q_copy(cc).wait_send()
    for t in range(n):
        for way, away in ((0, t > c), (1, t < c)):
            @pl.when(away)
            def _():
                for h in range(2):
                    z_sum(way, t, h).wait_send()


def fused(n, inputs, probe, cotangent, gate_weight, up_weight, down_weight):
    tokens, part = inputs.shape
    half, hidden = gate_weight.shape
    wide = 2 * half
    pieces = hidden // PIECE
    dma = pltpu.SemaphoreType.DMA
    any_spec = pl.BlockSpec(memory_space=pl.ANY)
    vmem = pltpu.VMEM
    out = pl.pallas_call(
        functools.partial(kernel, n),
        out_shape=jax.ShapeDtypeStruct((part, tokens), BF16),
        in_specs=[any_spec] * 6,
        out_specs=pl.BlockSpec(memory_space=pltpu.VMEM),
        scratch_shapes=[
            vmem((3, wide, tokens), BF16),
            vmem((2, 2 * tokens, half), BF16),
            vmem((2, tokens, half), BF16),
            vmem((half, hidden), BF16), vmem((half, hidden), BF16), vmem((hidden, half), BF16),
            vmem((half, hidden), BF16), vmem((half, hidden), BF16), vmem((hidden, half), BF16),
            vmem((wide, tokens), F32),
            vmem((n, part, tokens), BF16), vmem((n, part, tokens), BF16),
            vmem((n, part, tokens), BF16), vmem((2, n, part, tokens), BF16),
            dma((6,)),
            dma((pieces, 4)), dma((pieces, 4)), dma((pieces, 4)), dma((pieces, 4)),
            dma((n - 1,)), dma((n - 1,)), dma((n - 1,)), dma((n - 1,)),
            dma((n,)), dma((n,)), dma((n,)), dma((n,)),
            dma((n, 2)), dma((2, n, 2)),
        ],
        compiler_params=pltpu.CompilerParams(
            collective_id=0, has_side_effects=True, vmem_limit_bytes=60 * 2**20
        ),
        cost_estimate=pl.CostEstimate(
            flops=14 * tokens * wide * hidden,
            bytes_accessed=6 * half * hidden,
            transcendentals=tokens * hidden,
        ),
    )(inputs.T, probe.T, cotangent.T, gate_weight, up_weight, down_weight)
    return out.T


def gathered(inputs, probe, cotangent, gate_weight, up_weight, down_weight):
    gate_full, up_full, down_full = (
        lax.all_gather(gate_weight, "row", axis=0, tiled=True),
        lax.all_gather(up_weight, "row", axis=0, tiled=True),
        lax.all_gather(down_weight, "row", axis=1, tiled=True),
    )
    in_piece = lax.all_gather(inputs, ("col", "depth"), axis=1, tiled=True)
    probe_piece = lax.all_gather(probe, ("col", "depth"), axis=1, tiled=True)
    cot_piece = lax.all_gather(cotangent, ("col", "depth"), axis=1, tiled=True)
    pre_gate, pre_up = nn(in_piece, gate_full), nn(in_piece, up_full)
    tan_gate, tan_up = nn(probe_piece, gate_full), nn(probe_piece, up_full)
    back = nt(cot_piece, down_full)
    slope = gelu_slope(pre_gate)
    gate_part = (back * (tan_up * slope + pre_up * gelu_bend(pre_gate) * tan_gate)).astype(BF16)
    up_part = (back * slope * tan_gate).astype(BF16)
    term = nt(gate_part, gate_full) + nt(up_part, up_full)
    return lax.psum_scatter(
        term.astype(BF16), ("col", "depth"), scatter_dimension=1, tiled=True
    )


def solution(mesh):
    sizes = dict(mesh.shape)
    n = sizes["col"]

    def per_device(*args):
        half, hidden = args[3].shape
        square = sizes["groups"] == 2 and sizes["row"] == 2 and sizes["depth"] == 2
        even = half % 128 == 0 and hidden % PIECE == 0 and args[0].shape[1] % 32 == 0
        small = 2 * (n - 1) <= hidden // PIECE and half * hidden <= 2**21
        if square and even and small:
            return fused(n, *args)
        return gathered(*args)

    in_specs = (
        P(("groups", "row"), ("col", "depth")),
        P(("groups", "row"), ("col", "depth")),
        P(("groups", "row"), ("col", "depth")),
        P("row", ("col", "depth")),
        P("row", ("col", "depth")),
        P(("col", "depth"), "row"),
    )
    out_specs = P(("groups", "row"), ("col", "depth"))
    return jax.shard_map(
        per_device, mesh=mesh, in_specs=in_specs, out_specs=out_specs, check_vma=False
    )
```

```python
import functools

import jax
import jax.numpy as jnp
from jax import lax
from jax.experimental import pallas as pl
from jax.experimental.pallas import tpu as pltpu
from jax.sharding import PartitionSpec as P

MESH = pl.DeviceIdType.MESH
F32, BF16 = jnp.float32, jnp.bfloat16
K0, K1 = 0.7978845608, 0.044715
PIECE = 128
WIDE = 256


def gelu_tanh(value):
    return 0.5 * value * (1.0 + jnp.tanh(K0 * (value + K1 * value * value * value)))


def gelu_slope(value):
    return jax.jvp(gelu_tanh, (value,), (jnp.ones_like(value),))[1]


def gelu_bend(value):
    return jax.jvp(gelu_slope, (value,), (jnp.ones_like(value),))[1]


def slope_and_bend(s):
    sq = s * s
    t = jnp.tanh(K0 * s * (1.0 + K1 * sq))
    du = K0 + (3.0 * K0 * K1) * sq
    e = 1.0 - t * t
    slope = 0.5 * (1.0 + t) + 0.5 * s * e * du
    bend = e * (K0 + (6.0 * K0 * K1) * sq - s * t * du * du)
    return slope, bend


def nt(a, b):
    return lax.dot_general(a, b, (((1,), (1,)), ((), ())), preferred_element_type=F32)


def nn(a, b):
    return jnp.dot(a, b, preferred_element_type=F32)


def kernel(
    n, in_ref, pr_ref, ct_ref, gw_ref, uw_ref, dw_ref, out_ref,
    xt, xs, cot, own_g, own_u, own_d, far_g, far_u, far_d, acc,
    sib_out, sib_in, z_out, z_in,
    own_sem, xsend, xrecv, ysend, yrecv, rsend, rrecv, lsend, lrecv, ssend, srecv,
    qsend, qrecv, zsend, zrecv,
):
    g, r = lax.axis_index("groups"), lax.axis_index("row")
    c, d = lax.axis_index("col"), lax.axis_index("depth")
    half, hidden = gw_ref.shape
    part, tokens = in_ref.shape
    pieces = hidden // PIECE
    hd = half // 2

    def at(gg=g, rr=r, cc=c, dd=d):
        return (gg, rr, cc, dd)

    x_dev, y_dev, sib = at(rr=1 - r), at(gg=1 - g), at(dd=1 - d)

    def rows_of(cc, dd):
        return pl.ds(pl.multiple_of((cc * 2 + dd) * part, 32), part)

    own_copies = [
        pltpu.make_async_copy(gw_ref, own_g, own_sem.at[0]),
        pltpu.make_async_copy(uw_ref, own_u, own_sem.at[1]),
        pltpu.make_async_copy(dw_ref, own_d, own_sem.at[2]),
    ]
    raw_copies = [
        pltpu.make_async_copy(ref, xt.at[a, rows_of(c, d), :], own_sem.at[3 + a])
        for a, ref in enumerate((in_ref, pr_ref, ct_ref))
    ]
    for cp in raw_copies:
        cp.start()

    barrier = pltpu.get_barrier_semaphore()
    for dev in (x_dev, y_dev, sib):
        pl.semaphore_signal(barrier, inc=1, device_id=dev, device_id_type=MESH)
    for k in range(1, n):
        pl.semaphore_signal(
            barrier, inc=1, device_id=at(cc=lax.rem(c + k, n)), device_id_type=MESH
        )
    pl.semaphore_wait(barrier, n + 2)

    def windows(j, w):
        col = pl.ds(pl.multiple_of(j * PIECE, PIECE), PIECE)
        row = pl.ds(pl.multiple_of(w * hd, 32), hd)
        quarter = PIECE // 4
        first = pl.multiple_of(j * PIECE + w * (PIECE // 2), 64)
        second = pl.multiple_of(j * PIECE + w * (PIECE // 2) + quarter, 32)
        low, high = pl.ds(first, quarter), pl.ds(second, quarter)
        return (row, col), (row, col), (low, slice(None)), (high, slice(None))

    def x_copy(j, a):
        win = windows(j, g)[a]
        return pltpu.make_async_remote_copy(
            src_ref=(gw_ref, uw_ref, dw_ref, dw_ref)[a].at[win],
            dst_ref=(far_g, far_u, far_d, far_d)[a].at[win],
            send_sem=xsend.at[j, a], recv_sem=xrecv.at[j, a],
            device_id=x_dev, device_id_type=MESH,
        )

    def y_copy(j, a, w):
        win = windows(j, w)[a]
        far = (far_g, far_u, far_d, far_d)[a].at[win]
        return pltpu.make_async_remote_copy(
            src_ref=far, dst_ref=far,
            send_sem=ysend.at[j, a], recv_sem=yrecv.at[j, a],
            device_id=y_dev, device_id_type=MESH,
        )

    def x_start(j):
        for a in range(4):
            x_copy(j, a).start()

    def forward(j):
        for a in range(4):
            x_copy(j, a).wait_recv()
            y_copy(j, a, g).start()

    def forward_next(q):
        for a in range(4):
            @pl.when((q % 4 == a) & (q < 4 * pieces))
            def _():
                x_copy(q // 4, a).wait_recv()
                y_copy(q // 4, a, g).start()

    def y_arrived(j):
        for a in range(4):
            y_copy(j, a, 1 - g).wait_recv()

    def z_copy(s, right):
        src = c - s if right else c + s
        blk = xt.at[:, rows_of(src, d), :]
        return pltpu.make_async_remote_copy(
            src_ref=blk, dst_ref=blk,
            send_sem=(rsend if right else lsend).at[s],
            recv_sem=(rrecv if right else lrecv).at[s],
            device_id=at(cc=c + 1 if right else c - 1), device_id_type=MESH,
        )

    def z_arrival(s, right):
        src = c - 1 - s if right else c + 1 + s
        blk = xt.at[:, rows_of(src, d), :]
        return pltpu.make_async_remote_copy(
            src_ref=blk, dst_ref=blk,
            send_sem=(rsend if right else lsend).at[s],
            recv_sem=(rrecv if right else lrecv).at[s],
            device_id=at(cc=c - 1 if right else c + 1), device_id_type=MESH,
        )

    def sib_copy(src, dd=d):
        blk = xt.at[:, rows_of(src, dd), :]
        return pltpu.make_async_remote_copy(
            src_ref=blk, dst_ref=blk,
            send_sem=ssend.at[src], recv_sem=srecv.at[src],
            device_id=sib, device_id_type=MESH,
        )

    def sends(s, right):
        return (c + 1 < n) & (c - s >= 0) if right else (c >= 1) & (c + s < n)

    def gets(s, right):
        return c - 1 - s >= 0 if right else c + 1 + s < n

    def z_start(s, right):
        @pl.when(sends(s, right))
        def _():
            z_copy(s, right).start()

    def z_got(s, right):
        @pl.when(gets(s, right))
        def _():
            z_arrival(s, right).wait_recv()

        if s + 1 < n - 1:
            z_start(s + 1, right)

        @pl.when(gets(s, right))
        def _():
            sib_copy(c - 1 - s if right else c + 1 + s).start()

    for j in range(3):
        x_start(j)
    for a in range(3):
        raw_copies[a].wait()
    z_start(0, True)
    z_start(0, False)
    sib_copy(c).start()
    for cp in own_copies:
        cp.start()
    acc[...] = jnp.zeros_like(acc)

    blocks = half // 128

    def token_major(h):
        for src in range(n // 2):
            sib_copy(h * (n // 2) + src, dd=1 - d).wait_recv()

        @pl.loop(0, blocks)
        def _(j):
            feat = pl.ds(pl.multiple_of(h * half + j * 128, 128), 128)
            lane = pl.ds(pl.multiple_of(j * 128, 128), 128)
            xs[h, :tokens, lane] = xt[0, feat, :].T
            xs[h, tokens:, lane] = xt[1, feat, :].T
            cot[h, :, lane] = xt[2, feat, :].T

    side = (2 * c) // n
    near = n // 2 - 1
    lead = 2 * (n - 1)
    for j in range(lead):
        forward(j)
        if j + 3 < pieces:
            x_start(j + 3)
        if j % 2:
            z_got(j // 2, True)
            z_got(j // 2, False)
        if j == 2 * near:
            token_major(side)
    for cp in own_copies:
        cp.wait()
    token_major(1 - side)

    def forward_half(off, width, last=None):
        col = pl.ds(off, width)
        gates, ups = nn(xs[r], own_g[:, col]), nn(xs[r], own_u[:, col])
        back = nt(cot[r], own_d[col, :])
        if last is not None:
            y_copy(last, 0, 1 - g).wait_recv()
        gates = gates + nn(xs[1 - r], far_g[:, col])
        if last is not None:
            y_copy(last, 1, 1 - g).wait_recv()
        ups = ups + nn(xs[1 - r], far_u[:, col])
        if last is not None:
            y_copy(last, 2, 1 - g).wait_recv()
            y_copy(last, 3, 1 - g).wait_recv()
        back = back + nt(cot[1 - r], far_d[col, :])
        pre_gate, tan_gate = gates[:tokens], gates[tokens:]
        pre_up, tan_up = ups[:tokens], ups[tokens:]
        slope, bend = slope_and_bend(pre_gate)
        gate_part = (back * (tan_up * slope + pre_up * bend * tan_gate)).astype(BF16)
        up_part = (back * slope * tan_gate).astype(BF16)
        return gate_part, up_part

    def backward_half(off, width, gate_part, up_part, which=(0, 1)):
        col = pl.ds(off, width)
        for k in which:
            w_g, w_u, base = ((own_g, own_u, r), (far_g, far_u, 1 - r))[k]
            for q in range(0, half, part):
                rows = pl.ds(pl.multiple_of(base * half + q, 32), part)
                acc[rows, :] += nt(w_g[q:q + part, col], gate_part) + nt(
                    w_u[q:q + part, col], up_part
                )

    per = WIDE // PIECE
    steps = hidden // WIDE

    begin = 4 * lead + 1
    forward_next(begin - 1)

    @pl.loop(0, steps)
    def _(i):
        for k in range(per):
            y_arrived(i * per + k)
        off = pl.multiple_of(i * WIDE, WIDE)
        parts = forward_half(off, WIDE)
        forward_next(begin + 3 * i)
        forward_next(begin + 3 * i + 1)
        backward_half(off, WIDE, *parts)
        forward_next(begin + 3 * i + 2)

    for q in range(begin + 3 * steps, 4 * pieces):
        forward_next(q)
    def q_copy(cc):
        return pltpu.make_async_remote_copy(
            src_ref=sib_out.at[cc], dst_ref=sib_in.at[cc],
            send_sem=qsend.at[cc], recv_sem=qrecv.at[cc],
            device_id=sib, device_id_type=MESH,
        )

    def q_order(i):
        return (n - 1 - i) * (1 - side) + i * side

    def pair_send(i):
        t = q_order(i)
        sib_out[t] = acc[rows_of(t, 1 - d), :].astype(BF16)
        q_copy(t).start()

    tail = range(steps * per, pieces)
    for j in tail:
        off = j * PIECE
        parts = forward_half(off, PIECE, j)
        for k in range(2):
            @pl.when((r + 1 - side) % 2 == k)
            def _():
                backward_half(off, PIECE, *parts, which=(k,))
                if j == pieces - 1:
                    for i in range(n // 2):
                        pair_send(i)
                backward_half(off, PIECE, *parts, which=(1 - k,))
    for i in range(n // 2 if len(tail) else 0, n):
        pair_send(i)

    cut = part // 2

    def z_sum(way, t, h, back=False):
        rows = pl.ds(h * cut, cut)
        step = 1 - 2 * way
        return pltpu.make_async_remote_copy(
            src_ref=z_out.at[t, rows], dst_ref=z_in.at[way, t, rows],
            send_sem=zsend.at[t, h], recv_sem=zrecv.at[way, t, h],
            device_id=at(cc=c - step if back else c + step), device_id_type=MESH,
        )

    def shard(t, h):
        return pl.ds(pl.multiple_of((t * 2 + d) * part + h * cut, 16), cut)

    def add_in(way, t, h):
        @pl.when(c * (1 - way) + (n - 1 - c) * way > 0)
        def _():
            z_sum(way, t, h, back=True).wait_recv()
            acc[shard(t, h), :] += z_in[way, t, h * cut:(h + 1) * cut].astype(F32)

    def with_pair(t, h):
        other = sib_in[t, h * cut:(h + 1) * cut].astype(F32)
        return (acc[shard(t, h), :] + other).astype(BF16)

    def pass_on(way, t):
        @pl.when((t - c) * (1 - 2 * way) > 0)
        def _():
            for h in range(2):
                add_in(way, t, h)
                z_out[t, h * cut:(h + 1) * cut] = with_pair(t, h)
                z_sum(way, t, h).start()

    for i in range(n - 1):
        if i == 0:
            q_copy(q_order(0)).wait_recv()
        pass_on(side, q_order(i))
        if i == 0:
            for k in range(1, n):
                q_copy(q_order(k)).wait_recv()
        pass_on(1 - side, q_order(n - 1 - i))
    for h in range(2):
        add_in(side, c, h)
        add_in(1 - side, c, h)
        out_ref[h * cut:(h + 1) * cut, :] = with_pair(c, h)

    @pl.loop(0, pieces)
    def _(j):
        for a in range(4):
            x_copy(j, a).wait_send()
            y_copy(j, a, g).wait_send()

    for s in range(n - 1):
        for right in (True, False):
            @pl.when(sends(s, right))
            def _():
                z_copy(s, right).wait_send()
    for cc in range(n):
        sib_copy(cc).wait_send()
        q_copy(cc).wait_send()
    for t in range(n):
        for way, away in ((0, t > c), (1, t < c)):
            @pl.when(away)
            def _():
                for h in range(2):
                    z_sum(way, t, h).wait_send()


def fused(n, inputs, probe, cotangent, gate_weight, up_weight, down_weight):
    tokens, part = inputs.shape
    half, hidden = gate_weight.shape
    wide = 2 * half
    pieces = hidden // PIECE
    dma = pltpu.SemaphoreType.DMA
    any_spec = pl.BlockSpec(memory_space=pl.ANY)
    vmem = pltpu.VMEM
    out = pl.pallas_call(
        functools.partial(kernel, n),
        out_shape=jax.ShapeDtypeStruct((part, tokens), BF16),
        in_specs=[any_spec] * 6,
        out_specs=pl.BlockSpec(memory_space=pltpu.VMEM),
        scratch_shapes=[
            vmem((3, wide, tokens), BF16),
            vmem((2, 2 * tokens, half), BF16),
            vmem((2, tokens, half), BF16),
            vmem((half, hidden), BF16), vmem((half, hidden), BF16), vmem((hidden, half), BF16),
            vmem((half, hidden), BF16), vmem((half, hidden), BF16), vmem((hidden, half), BF16),
            vmem((wide, tokens), F32),
            vmem((n, part, tokens), BF16), vmem((n, part, tokens), BF16),
            vmem((n, part, tokens), BF16), vmem((2, n, part, tokens), BF16),
            dma((6,)),
            dma((pieces, 4)), dma((pieces, 4)), dma((pieces, 4)), dma((pieces, 4)),
            dma((n - 1,)), dma((n - 1,)), dma((n - 1,)), dma((n - 1,)),
            dma((n,)), dma((n,)), dma((n,)), dma((n,)),
            dma((n, 2)), dma((2, n, 2)),
        ],
        compiler_params=pltpu.CompilerParams(
            collective_id=0, has_side_effects=True, vmem_limit_bytes=60 * 2**20
        ),
        cost_estimate=pl.CostEstimate(
            flops=14 * tokens * wide * hidden,
            bytes_accessed=6 * half * hidden,
            transcendentals=tokens * hidden,
        ),
    )(inputs.T, probe.T, cotangent.T, gate_weight, up_weight, down_weight)
    return out.T


def gathered(inputs, probe, cotangent, gate_weight, up_weight, down_weight):
    gate_full, up_full, down_full = (
        lax.all_gather(gate_weight, "row", axis=0, tiled=True),
        lax.all_gather(up_weight, "row", axis=0, tiled=True),
        lax.all_gather(down_weight, "row", axis=1, tiled=True),
    )
    in_piece = lax.all_gather(inputs, ("col", "depth"), axis=1, tiled=True)
    probe_piece = lax.all_gather(probe, ("col", "depth"), axis=1, tiled=True)
    cot_piece = lax.all_gather(cotangent, ("col", "depth"), axis=1, tiled=True)
    pre_gate, pre_up = nn(in_piece, gate_full), nn(in_piece, up_full)
    tan_gate, tan_up = nn(probe_piece, gate_full), nn(probe_piece, up_full)
    back = nt(cot_piece, down_full)
    slope = gelu_slope(pre_gate)
    gate_part = (back * (tan_up * slope + pre_up * gelu_bend(pre_gate) * tan_gate)).astype(BF16)
    up_part = (back * slope * tan_gate).astype(BF16)
    term = nt(gate_part, gate_full) + nt(up_part, up_full)
    return lax.psum_scatter(
        term.astype(BF16), ("col", "depth"), scatter_dimension=1, tiled=True
    )


def solution(mesh):
    sizes = dict(mesh.shape)
    n = sizes["col"]

    def per_device(*args):
        half, hidden = args[3].shape
        square = sizes["groups"] == 2 and sizes["row"] == 2 and sizes["depth"] == 2
        even = half % 128 == 0 and hidden % PIECE == 0 and args[0].shape[1] % 32 == 0
        small = 2 * (n - 1) <= hidden // PIECE and half * hidden <= 2**21
        if square and even and small:
            return fused(n, *args)
        return gathered(*args)

    in_specs = (
        P(("groups", "row"), ("col", "depth")),
        P(("groups", "row"), ("col", "depth")),
        P(("groups", "row"), ("col", "depth")),
        P("row", ("col", "depth")),
        P("row", ("col", "depth")),
        P(("col", "depth"), "row"),
    )
    out_specs = P(("groups", "row"), ("col", "depth"))
    return jax.shard_map(
        per_device, mesh=mesh, in_specs=in_specs, out_specs=out_specs, check_vma=False
    )
```
